256 devices in a mesh: prow: 32 (over z_hi, x, y), pcol: 8 (over z_lo, core).
Axes of the slice: x: 4, y: 4, z: 8 (z_hi: 2, z_lo: 4; z = z_hi * 4 + z_lo), core: 2. Of those that a mesh axis runs over, the one named last changes fastest.
Arguments:
- ancestor_inverse: bfloat16 [20480, 20480], P('prow', 'pcol'), may hold values from -6 to 6
- lower_panel: bfloat16 [2, 20480, 512], P(None, 'pcol'), may hold values from -0.0625 to 0.0625
- pattern: int32 [2, 80], replicated, may hold values from 0 to 159, as said below
- diag_inverse: float32 [2, 512, 512], P(None, ('prow', 'pcol')), may hold values from -6 to 6
Outputs:
- off_diagonal: bfloat16 [2, 20480, 512], P(None, ('prow', 'pcol'))
- diagonal_block: float32 [2, 512, 512], P(None, ('prow', 'pcol'))
The draws below stay inside these ranges and needn't reach their ends.
Inputs may be any that keep to these rules, and one draw needn't show every extreme that they name: `pattern`: each row lists 80 distinct block indices in increasing order, the first 0 and the last 159.
All inputs are finite; a program needn't handle non-finite values.
Results may differ from the reference program's by a relative error of at most 0.0095.
Values may be sent and summed in bfloat16 or wider, within the bound.
No kernel may reach another device: no remote copies, remote signals or barrier semaphores. Data moves between devices by JAX's collectives and lax.ppermute only.
A program may use at most 64 MiB of HBM per device.

```python
import jax
import jax.numpy as jnp
from jax import lax

BLOCK = 128
W = 512
NB = 160
NS = 80
N = 20480


def draw_pattern(key, part):
    key = jax.random.fold_in(key, 5)
    listed = []
    for member in range(2):
        shuffled = jax.random.permutation(jax.random.fold_in(key, member), NB - 2) + 1
        picked = jnp.sort(shuffled[:NS - 2])
        head = jnp.zeros((1,), jnp.int32)
        tail = jnp.full((1,), NB - 1, jnp.int32)
        listed.append(jnp.concatenate([head, picked.astype(jnp.int32), tail]))
    return jnp.stack(listed).astype(jnp.int32)


def shard_levels(rng, extent, cuts, low, top_value):
    def one(dim, shards_of):
        draws = jax.random.uniform(jax.random.fold_in(jax.random.fold_in(rng, 6), dim), (shards_of,), jnp.float32, low / len(cuts), top_value / len(cuts))
        return jnp.repeat(jnp.exp(draws), extent[dim] // shards_of).reshape((-1,) + (1,) * (len(extent) - dim - 1))

    level = one(*cuts[0])
    for cut in cuts[1:]:
        level = level * one(*cut)
    return level


def gaussian(rng, shape, width, reach, cuts=(), kind=jnp.bfloat16):
    result = jax.random.normal(rng, shape, jnp.float32) * width
    if len(cuts) > 0:
        result = shard_levels(rng, shape, cuts, -0.22, 0.18) * result
    return jnp.clip(result, min=-reach, max=reach).astype(kind)


def setup_inputs(seed: int = 0) -> dict:
    keys = jax.random.split(jax.random.key(seed), 5)
    ancestor_inverse = gaussian(keys[0], (N, N), 1.0, 6.0, ((0, 32), (1, 8)))
    lower_panel = gaussian(keys[1], (2, N, W), (NS * BLOCK) ** -0.5, 0.0625, ((1, 8),))
    pattern = draw_pattern(jax.random.fold_in(keys[4], 71), 0)
    diag_inverse = gaussian(keys[3], (2, W, W), 1.0, 6.0, ((1, 256),), jnp.float32)
    return {"ancestor_inverse": ancestor_inverse, "lower_panel": lower_panel, "pattern": pattern, "diag_inverse": diag_inverse}


def block_mask(pattern, height):
    block_ids = jnp.arange(height, dtype=jnp.int32) // BLOCK
    return jnp.any(pattern[:, :, None] == block_ids[None, None, :], axis=1)


def reference(ancestor_inverse, lower_panel, pattern, diag_inverse):
    height = ancestor_inverse.shape[0]
    selected = block_mask(pattern, height)
    masked = lower_panel * selected[:, :, None].astype(lower_panel.dtype)
    joined = jnp.concatenate([masked[0], masked[1]], axis=1)
    slabs = ancestor_inverse.reshape(height // BLOCK, BLOCK, height)

    def one_slab(slab):
        return jnp.dot(slab, joined, preferred_element_type=jnp.float32)

    product = lax.map(one_slab, slabs).reshape(height, 2 * W)
    product_pair = jnp.stack([product[:, :W], product[:, W:]])
    off_diagonal = (-(product_pair * selected[:, :, None].astype(jnp.float32))).astype(jnp.bfloat16)
    diagonal_block = diag_inverse + jnp.einsum("sna,snb->sab", masked.astype(jnp.float32), product_pair, precision=lax.Precision.HIGHEST)
    return off_diagonal, diagonal_block
```

```python
import jax
import jax.numpy as jnp
import numpy as np
from jax import lax
from jax.experimental import pallas as pl
from jax.experimental.pallas import tpu as pltpu
from jax.sharding import Mesh
from jax.sharding import PartitionSpec as P

BLOCK = 128
VMEM = pltpu.VMEM
BF16 = jnp.bfloat16
F32 = jnp.float32


def params(**kw):
    return pltpu.CompilerParams(vmem_limit_bytes=40 * 1024 * 1024, **kw)


def whole():
    return pl.BlockSpec(memory_space=VMEM)


def scalars():
    return pl.BlockSpec(memory_space=pltpu.SMEM)


def product(place, ancestor, panel, pattern, kind):
    height, breadth = ancestor.shape
    wide = panel.shape[2]
    step = 512
    steps = breadth // step

    def kernel(place_ref, a_ref, l_ref, p_ref, o_ref, acc):
        k = pl.program_id(0)
        row = p_ref[pl.ds(place_ref[0], 1), :]
        first = place_ref[1] + k * (step // BLOCK)
        parts = []
        for b in range(step // BLOCK):
            hit = jnp.max(jnp.where(row == first + b, 1.0, 0.0).astype(F32), axis=1, keepdims=True)
            parts.append(l_ref[0, b * BLOCK : (b + 1) * BLOCK, :] * hit.astype(BF16))
        masked = jnp.concatenate(parts, axis=0)
        term = jnp.dot(a_ref[...], masked, preferred_element_type=F32)

        @pl.when(k == 0)
        def _():
            acc[...] = term

        @pl.when(jnp.logical_and(k > 0, k < steps - 1))
        def _():
            acc[...] += term

        @pl.when(k == steps - 1)
        def _():
            o_ref[...] = (acc[...] + term).astype(kind)

    return pl.pallas_call(
        kernel,
        grid_spec=pltpu.PrefetchScalarGridSpec(
            num_scalar_prefetch=1,
            grid=(steps,),
            in_specs=[
                pl.BlockSpec((height, step), lambda k, at: (0, k)),
                pl.BlockSpec((1, step, wide), lambda k, at: (at[0], k, 0)),
                pl.BlockSpec(pattern.shape, lambda k, at: (0, 0)),
            ],
            out_specs=pl.BlockSpec((height, wide), lambda k, at: (0, 0)),
            scratch_shapes=[pltpu.VMEM((height, wide), F32)],
        ),
        out_shape=jax.ShapeDtypeStruct((height, wide), kind),
        compiler_params=params(),
        cost_estimate=pl.CostEstimate(
            flops=2 * height * breadth * wide,
            bytes_accessed=2 * (height * breadth + breadth * wide + height * wide),
            transcendentals=0,
        ),
        name="product",
    )(place, ancestor, panel, pattern)


def join(place, own, arrived, lines):
    height, wide = own.shape
    part = height // lines

    def kernel(place_ref, own_ref, in_ref, keep_ref, *sent):
        here = place_ref[0]
        for m in range(lines):
            rows = pl.ds(pl.multiple_of((here ^ m) * part, 16), part)
            total = own_ref[rows, :] + in_ref[rows, :].astype(F32)
            if m == 0:
                keep_ref[...] = total
            else:
                sent[m - 1][...] = total.astype(BF16)

    piece = jax.ShapeDtypeStruct((part, wide), BF16)
    return pl.pallas_call(
        kernel,
        in_specs=[scalars(), whole(), whole()],
        out_specs=[whole()] * lines,
        out_shape=[jax.ShapeDtypeStruct((part, wide), F32)] + [piece] * (lines - 1),
        compiler_params=params(),
        name="join",
    )(place, own, arrived)


def contract(place, pattern, mine, keep, arrived):
    part, wide = keep.shape
    half = part // 2

    def kernel(place_ref, p_ref, m_ref, keep_ref, *rest):
        ins, (own_ref, send_ref, g_ref, off) = rest[: len(arrived)], rest[len(arrived) :]
        total = keep_ref[...]
        for r in ins:
            total = total + r[...].astype(F32)
        row = p_ref[pl.ds(place_ref[0], 1), :]
        ids = (place_ref[1] + lax.broadcasted_iota(jnp.int32, (part, 1), 0)) >> 7
        hit = jnp.max(jnp.where(ids == row, 1.0, 0.0).astype(F32), axis=1, keepdims=True)
        off[...] = -(total * hit)
        core = place_ref[2]
        own_ref[...] = off[pl.ds(pl.multiple_of(core * half, 16), half), :].astype(BF16)
        send_ref[...] = off[pl.ds(pl.multiple_of((1 - core) * half, 16), half), :].astype(BF16)
        masked = m_ref[...] * hit.astype(BF16)
        g = lax.dot_general(masked, total.astype(BF16), (((0,), (0,)), ((), ())), preferred_element_type=F32)
        g_ref[...] = g.astype(BF16)

    piece = jax.ShapeDtypeStruct((half, wide), BF16)
    return pl.pallas_call(
        kernel,
        in_specs=[scalars()] + [whole()] * (3 + len(arrived)),
        out_specs=[whole()] * 3,
        out_shape=[piece, piece, jax.ShapeDtypeStruct((wide, wide), BF16)],
        scratch_shapes=[pltpu.VMEM((part, wide), F32)],
        compiler_params=params(),
        name="contract",
    )(place, pattern, mine, keep, *arrived)


def solution(mesh):
    cut = Mesh(mesh.devices.reshape(2, 4, 4, 4, 2), ("zh", "x", "y", "zl", "c"))
    every = ("zh", "x", "y", "zl", "c")
    xor4 = {m: [(i, i ^ m) for i in range(4)] for m in (1, 2, 3)}
    swap = [(0, 1), (1, 0)]
    fetch = []
    for zh in range(2):
        for x in range(4):
            for y in range(4):
                for p in range(8):
                    source = ((zh * 4 + x) * 4 + y) * 8 + p
                    fetch.append((source, (p * 4 + y) * 8 + (2 * zh + (x >> 1)) * 2 + (x & 1)))

    def local(ancestor, panel, pattern, diag):
        height, breadth = ancestor.shape
        wide = panel.shape[2]
        zh, x, y, zl, c = (lax.axis_index(a) for a in every)
        part = height // 4
        columns = (zl * 2 + c) * (breadth // BLOCK)
        first = ((zh * 4 + x) * 4 + y) * height + zl * part

        fetched = lax.dynamic_slice(
            panel, (x & 1, y * height + (2 * zh + (x >> 1)) * part, 0), (1, part, wide)
        )[0]
        mine = lax.ppermute(fetched, every, fetch)

        other = product(jnp.stack([1 - c, columns]), ancestor, panel, pattern, BF16)
        swapped = lax.ppermute(other, "c", swap)
        own = product(jnp.stack([c, columns]), ancestor, panel, pattern, F32)
        keep, *sent = join(jnp.stack([zl]), own, swapped, 4)
        arrived = [lax.ppermute(sent[m - 1], "zl", xor4[m]) for m in (3, 2, 1)]
        off_own, off_send, g = contract(jnp.stack([c, first, c]), pattern, mine, keep, arrived)
        off_other = lax.ppermute(off_send, "c", swap)
        off = jnp.where(c == 0, jnp.stack([off_own, off_other]), jnp.stack([off_other, off_own]))
        pieces = lax.all_to_all(g.reshape(256, 2, wide), every, 0, 0, tiled=True)
        total = jnp.sum(pieces.reshape(128, 2, 2, wide).astype(F32), axis=0)
        return off, diag + total

    rows = ("zh", "x", "y")
    cols = ("zl", "c")
    return jax.shard_map(
        local,
        mesh=cut,
        in_specs=(P(rows, cols), P(None, cols, None), P(), P(None, every, None)),
        out_specs=(P(None, every, None), P(None, every, None)),
        check_vma=False,
    )
```

```python
import jax
import jax.numpy as jnp
import numpy as np
from jax import lax
from jax.experimental import pallas as pl
from jax.experimental.pallas import tpu as pltpu
from jax.sharding import Mesh
from jax.sharding import PartitionSpec as P

BLOCK = 128
VMEM = pltpu.VMEM
BF16 = jnp.bfloat16
F32 = jnp.float32


def params(mib=40):
    return pltpu.CompilerParams(vmem_limit_bytes=mib * 1024 * 1024)


def whole():
    return pl.BlockSpec(memory_space=VMEM)


def scalars():
    return pl.BlockSpec(memory_space=pltpu.SMEM)


def place_of(me):
    return me >> 7, (me >> 5) & 3, (me >> 3) & 3, (me >> 1) & 3, me & 1


def masked(rows, pattern_row, first):
    parts = []
    for b in range(rows.shape[0] // BLOCK):
        hit = jnp.max(jnp.where(pattern_row == first + b, 1.0, 0.0).astype(F32), axis=1, keepdims=True)
        parts.append(rows[b * BLOCK : (b + 1) * BLOCK, :] * hit.astype(BF16))
    return jnp.concatenate(parts, axis=0)


def hbm():
    return pl.BlockSpec(memory_space=pltpu.HBM)


STEP = 512
LIMIT = 50


def cost(height, breadth, wide):
    return pl.CostEstimate(
        flops=2 * height * breadth * wide,
        bytes_accessed=2 * (height * breadth + breadth * wide + height * wide),
        transcendentals=0,
    )


def products(me, ancestor, panel, pattern):
    height, breadth = ancestor.shape
    wide = panel.shape[2]
    steps = breadth // STEP
    part = height // 4

    def kernel(me_ref, a_hbm, l_hbm, p_hbm, o_ref, k_ref, f_ref, p_ref, a_buf, l_buf, acc, a_sem, l_sem, f_sem, p_sem):
        zh, x, y, zl, c = place_of(me_ref[0])
        listed = pltpu.make_async_copy(p_hbm, p_ref, p_sem)
        listed.start()
        order = (1 - c, c)
        a_copies, l_copies = [], []
        for k in range(steps):
            cols = pl.ds(k * STEP, STEP)
            a_copies.append(pltpu.make_async_copy(a_hbm.at[:, cols], a_buf.at[k], a_sem.at[k]))
            l_copies.append(
                [
                    pltpu.make_async_copy(l_hbm.at[order[i], cols, :], l_buf.at[i, k], l_sem.at[i, k])
                    for i in range(2)
                ]
            )
            a_copies[k].start()
            l_copies[k][0].start()
            l_copies[k][1].start()
        start = pl.multiple_of(y * height + (2 * zh + (x >> 1)) * part, 16)
        fetch = pltpu.make_async_copy(l_hbm.at[x & 1, pl.ds(start, part), :], f_ref, f_sem)
        fetch.start()
        listed.wait()
        first = (zl * 2 + c) * (breadth // BLOCK)
        for k in range(steps):
            a_copies[k].wait()
            for i in range(2):
                l_copies[k][i].wait()
                row = p_ref[pl.ds(order[i], 1), :]
                rows = masked(l_buf[i, k], row, first + k * (STEP // BLOCK))
                term = jnp.dot(a_buf[k], rows, preferred_element_type=F32)
                total = acc if i == 0 else k_ref
                if k == 0:
                    total[...] = term
                elif k == steps - 1 and i == 0:
                    o_ref[...] = (total[...] + term).astype(BF16)
                else:
                    total[...] += term
        fetch.wait()

    return pl.pallas_call(
        kernel,
        in_specs=[scalars(), hbm(), hbm(), hbm()],
        out_specs=[whole(), whole(), whole()],
        out_shape=[
            jax.ShapeDtypeStruct((height, wide), BF16),
            jax.ShapeDtypeStruct((height, wide), F32),
            jax.ShapeDtypeStruct((part, wide), BF16),
        ],
        scratch_shapes=[
            pltpu.VMEM(pattern.shape, pattern.dtype),
            pltpu.VMEM((steps, height, STEP), BF16),
            pltpu.VMEM((2, steps, STEP, wide), BF16),
            pltpu.VMEM((height, wide), F32),
            pltpu.SemaphoreType.DMA((steps,)),
            pltpu.SemaphoreType.DMA((2, steps)),
            pltpu.SemaphoreType.DMA,
            pltpu.SemaphoreType.DMA,
        ],
        compiler_params=params(LIMIT),
        cost_estimate=cost(height, breadth, 2 * wide),
        name="products",
    )(me, ancestor, panel, pattern)


def join(me, own, arrived, lines):
    height, wide = own.shape
    part = height // lines

    def kernel(me_ref, own_ref, in_ref, keep_ref, *sent):
        here = place_of(me_ref[0])[3]
        for m in range(lines):
            rows = pl.ds(pl.multiple_of((here ^ m) * part, 16), part)
            total = own_ref[rows, :] + in_ref[rows, :].astype(F32)
            if m == 0:
                keep_ref[...] = total
            else:
                sent[m - 1][...] = total.astype(BF16)

    piece = jax.ShapeDtypeStruct((part, wide), BF16)
    return pl.pallas_call(
        kernel,
        in_specs=[scalars(), whole(), whole()],
        out_specs=[whole()] * lines,
        out_shape=[jax.ShapeDtypeStruct((part, wide), F32)] + [piece] * (lines - 1),
        compiler_params=params(),
        name="join",
    )(me, own, arrived)


def contract(me, height, pattern, mine, keep, arrived):
    part, wide = keep.shape
    half = part // 2

    def kernel(me_ref, p_ref, m_ref, keep_ref, *rest):
        zh, x, y, zl, core = place_of(me_ref[0])
        first = ((zh * 4 + x) * 4 + y) * height + zl * part
        ins, (own_ref, send_ref, g_ref, off) = rest[: len(arrived)], rest[len(arrived) :]
        total = keep_ref[...]
        for r in ins:
            total = total + r[...].astype(F32)
        row = p_ref[pl.ds(core, 1), :]
        ids = (first + lax.broadcasted_iota(jnp.int32, (part, 1), 0)) >> 7
        hit = jnp.max(jnp.where(ids == row, 1.0, 0.0).astype(F32), axis=1, keepdims=True)
        off[...] = -(total * hit)
        own_ref[...] = off[pl.ds(pl.multiple_of(core * half, 16), half), :].astype(BF16)
        send_ref[...] = off[pl.ds(pl.multiple_of((1 - core) * half, 16), half), :].astype(BF16)
        chosen = m_ref[...] * hit.astype(BF16)
        g = lax.dot_general(chosen, total.astype(BF16), (((0,), (0,)), ((), ())), preferred_element_type=F32)
        g = g.astype(BF16)
        groups, both = g_ref.shape[0], g_ref.shape[1] // 2
        for i in range(groups):
            for h in range(2):
                start = h * (wide // 2) + i * both
                g_ref[i, h * both : (h + 1) * both, :] = g[start : start + both, :]

    piece = jax.ShapeDtypeStruct((half, wide), BF16)
    return pl.pallas_call(
        kernel,
        in_specs=[scalars()] + [whole()] * (3 + len(arrived)),
        out_specs=[whole()] * 3,
        out_shape=[piece, piece, jax.ShapeDtypeStruct((16, wide // 16, wide), BF16)],
        scratch_shapes=[pltpu.VMEM((part, wide), F32)],
        compiler_params=params(),
        name="contract",
    )(me, pattern, mine, keep, *arrived)


def gather(pieces):
    count, tall, wide = pieces.shape

    def kernel(in_ref, o_ref):
        total = in_ref[0].astype(F32)
        for i in range(1, count):
            total = total + in_ref[i].astype(F32)
        for j in range(tall // 2):
            o_ref[j] = total[2 * j : 2 * j + 2, :].astype(o_ref.dtype)

    return pl.pallas_call(
        kernel,
        in_specs=[whole()],
        out_specs=whole(),
        out_shape=jax.ShapeDtypeStruct((tall // 2, 2, wide), F32),
        compiler_params=params(),
        name="gather",
    )(pieces)


def finish(pieces, diag):
    def kernel(in_ref, d_ref, o_ref):
        for s in range(2):
            total = in_ref[s]
            for i in range(s + 2, in_ref.shape[0], 2):
                total = total + in_ref[i]
            o_ref[s] = d_ref[s] + total

    return pl.pallas_call(
        kernel,
        in_specs=[whole(), whole()],
        out_specs=whole(),
        out_shape=jax.ShapeDtypeStruct(diag.shape, F32),
        compiler_params=params(),
        name="finish",
    )(pieces, diag)


def solution(mesh):
    cut = Mesh(mesh.devices.reshape(2, 4, 4, 4, 2), ("zh", "x", "y", "zl", "c"))
    every = ("zh", "x", "y", "zl", "c")
    xor4 = {m: [(i, i ^ m) for i in range(4)] for m in (1, 2, 3)}
    swap = [(0, 1), (1, 0)]
    fetch = []
    for zh in range(2):
        for x in range(4):
            for y in range(4):
                for p in range(8):
                    source = ((zh * 4 + x) * 4 + y) * 8 + p
                    fetch.append((source, (p * 4 + y) * 8 + (2 * zh + (x >> 1)) * 2 + (x & 1)))

    def local(ancestor, panel, pattern, diag):
        me = jnp.reshape(lax.axis_index(every), (1,))
        core = lax.axis_index("c")
        other, own, fetched = products(me, ancestor, panel, pattern)
        swapped = lax.ppermute(other, "c", swap)
        mine = lax.ppermute(fetched, every, fetch)
        keep, *sent = join(me, own, swapped, 4)
        arrived = [lax.ppermute(sent[m - 1], "zl", xor4[m]) for m in (3, 2, 1)]
        off_own, off_send, g = contract(me, ancestor.shape[0], pattern, mine, keep, arrived)
        pieces = lax.all_to_all(g, ("x", "y"), 0, 0, tiled=True)
        off_other = lax.ppermute(off_send, "c", swap)
        off = jnp.where(core == 0, jnp.stack([off_own, off_other]), jnp.stack([off_other, off_own]))
        pieces = lax.all_to_all(gather(pieces), ("zh", "zl", "c"), 0, 0, tiled=True)
        return off, finish(pieces, diag)

    rows = ("zh", "x", "y")
    cols = ("zl", "c")
    return jax.shard_map(
        local,
        mesh=cut,
        in_specs=(P(rows, cols), P(None, cols, None), P(), P(None, every, None)),
        out_specs=(P(None, every, None), P(None, every, None)),
        check_vma=False,
    )
```

```python
import jax
import jax.numpy as jnp
import numpy as np
from jax import lax
from jax.experimental import pallas as pl
from jax.experimental.pallas import tpu as pltpu
from jax.sharding import Mesh
from jax.sharding import PartitionSpec as P

BLOCK = 128
VMEM = pltpu.VMEM
BF16 = jnp.bfloat16
F32 = jnp.float32


def params(mib=40):
    return pltpu.CompilerParams(vmem_limit_bytes=mib * 1024 * 1024)


def whole():
    return pl.BlockSpec(memory_space=VMEM)


def scalars():
    return pl.BlockSpec(memory_space=pltpu.SMEM)


def place_of(me):
    return me >> 7, (me >> 5) & 3, (me >> 3) & 3, (me >> 1) & 3, me & 1


def masked(rows, pattern_row, first):
    parts = []
    for b in range(rows.shape[0] // BLOCK):
        hit = jnp.max(jnp.where(pattern_row == first + b, 1.0, 0.0).astype(F32), axis=1, keepdims=True)
        parts.append(rows[b * BLOCK : (b + 1) * BLOCK, :] * hit.astype(BF16))
    return jnp.concatenate(parts, axis=0)


def hbm():
    return pl.BlockSpec(memory_space=pltpu.HBM)


STEP = 512
LIMIT = 50
ROUTES = (
    (1, 4, 2, 3, 7, 6, 5, 0),
    (4, 3, 2, 1, 0, 5, 7, 6),
    (3, 5, 4, 2, 7, 0, 6, 1),
    (4, 2, 3, 5, 1, 6, 0, 7),
    (1, 7, 6, 0, 2, 5, 4, 3),
    (7, 1, 0, 6, 4, 2, 3, 5),
    (0, 2, 6, 1, 5, 4, 7, 3),
    (1, 7, 0, 2, 6, 3, 5, 4),
)


def cost(height, breadth, wide):
    return pl.CostEstimate(
        flops=2 * height * breadth * wide,
        bytes_accessed=2 * (height * breadth + breadth * wide + height * wide),
        transcendentals=0,
    )


def products(me, ancestor, panel, pattern):
    height, breadth = ancestor.shape
    wide = panel.shape[2]
    steps = breadth // STEP

    def kernel(me_ref, a_hbm, l_hbm, p_hbm, o_ref, k_ref, p_ref, a_buf, l_buf, acc, a_sem, l_sem, p_sem):
        zh, x, y, zl, c = place_of(me_ref[0])
        listed = pltpu.make_async_copy(p_hbm, p_ref, p_sem)
        listed.start()
        order = (1 - c, c)
        a_copies, l_copies = [], []
        for k in range(steps):
            cols = pl.ds(k * STEP, STEP)
            a_copies.append(pltpu.make_async_copy(a_hbm.at[:, cols], a_buf.at[k], a_sem.at[k]))
            l_copies.append(
                [
                    pltpu.make_async_copy(l_hbm.at[order[i], cols, :], l_buf.at[i, k], l_sem.at[i, k])
                    for i in range(2)
                ]
            )
            a_copies[k].start()
            l_copies[k][0].start()
            l_copies[k][1].start()
        listed.wait()
        first = (zl * 2 + c) * (breadth // BLOCK)
        for k in range(steps):
            a_copies[k].wait()
            for i in range(2):
                l_copies[k][i].wait()
                row = p_ref[pl.ds(order[i], 1), :]
                rows = masked(l_buf[i, k], row, first + k * (STEP // BLOCK))
                term = jnp.dot(a_buf[k], rows, preferred_element_type=F32)
                total = acc if i == 0 else k_ref
                if k == 0:
                    total[...] = term
                elif k == steps - 1 and i == 0:
                    o_ref[...] = (total[...] + term).astype(BF16)
                else:
                    total[...] += term

    return pl.pallas_call(
        kernel,
        in_specs=[scalars(), hbm(), hbm(), hbm()],
        out_specs=[whole(), whole()],
        out_shape=[
            jax.ShapeDtypeStruct((height, wide), BF16),
            jax.ShapeDtypeStruct((height, wide), F32),
        ],
        scratch_shapes=[
            pltpu.VMEM(pattern.shape, pattern.dtype),
            pltpu.VMEM((steps, height, STEP), BF16),
            pltpu.VMEM((2, steps, STEP, wide), BF16),
            pltpu.VMEM((height, wide), F32),
            pltpu.SemaphoreType.DMA((steps,)),
            pltpu.SemaphoreType.DMA((2, steps)),
            pltpu.SemaphoreType.DMA,
        ],
        compiler_params=params(LIMIT),
        cost_estimate=cost(height, breadth, 2 * wide),
        name="products",
    )(me, ancestor, panel, pattern)


def pick(me, height, panel):
    part, wide = height // 4, panel.shape[2]

    def kernel(me_ref, l_hbm, f_ref, sem):
        zh, x, y, zl, c = place_of(me_ref[0])
        code = jnp.int32(0)
        for p, row in enumerate(ROUTES):
            code = jnp.where(zl * 2 + c == p, sum(v << (3 * q) for q, v in enumerate(row)), code)
        to = (code >> (3 * (zh * 4 + x))) & 7
        copies = []
        for m in range(2):
            start = pl.multiple_of(y * height + ((to >> 1) ^ (2 * m)) * part, 16)
            copies.append(
                pltpu.make_async_copy(
                    l_hbm.at[to & 1, pl.ds(start, part), :], f_ref.at[pl.ds(m * part, part), :], sem.at[m]
                )
            )
            copies[m].start()
        for copy in copies:
            copy.wait()

    return pl.pallas_call(
        kernel,
        in_specs=[scalars(), hbm()],
        out_specs=hbm(),
        out_shape=jax.ShapeDtypeStruct((2 * part, wide), panel.dtype),
        scratch_shapes=[pltpu.SemaphoreType.DMA((2,))],
        compiler_params=params(LIMIT),
        name="pick",
    )(me, panel)


def join(me, own, arrived):
    height, wide = own.shape
    part = height // 4

    def kernel(me_ref, own_ref, in_ref, near_ref, far_ref, sent_ref):
        here = place_of(me_ref[0])[3]
        for m in range(4):
            rows = pl.ds(pl.multiple_of((here ^ m) * part, 16), part)
            total = own_ref[rows, :] + in_ref[rows, :].astype(F32)
            if m == 0:
                near_ref[...] = total
            elif m == 2:
                far_ref[...] = total
            else:
                sent_ref[(m // 2) * part : (m // 2 + 1) * part, :] = total.astype(BF16)

    piece = jax.ShapeDtypeStruct((part, wide), F32)
    return pl.pallas_call(
        kernel,
        in_specs=[scalars(), whole(), whole()],
        out_specs=[whole()] * 3,
        out_shape=[piece, piece, jax.ShapeDtypeStruct((2 * part, wide), BF16)],
        compiler_params=params(),
        name="join",
    )(me, own, arrived)


def chosen(first, count, pattern_row):
    ids = (first + lax.broadcasted_iota(jnp.int32, (count, 1), 0)) >> 7
    return jnp.max(jnp.where(ids == pattern_row, 1.0, 0.0).astype(F32), axis=1, keepdims=True)


def contract(me, height, pattern, mine, near, far, arrived):
    part, wide = near.shape

    def kernel(me_ref, p_ref, m_ref, near_ref, far_ref, in_ref, half_ref, sent_ref, g_ref, m_buf, s_buf):
        zh, x, y, zl, core = place_of(me_ref[0])
        row = p_ref[pl.ds(core, 1), :]
        base = ((zh * 4 + x) * 4 + y) * height
        near_sum = near_ref[...] + in_ref[:part, :].astype(F32)
        half_ref[...] = near_sum
        far_sum = (far_ref[...] + in_ref[part:, :].astype(F32)).astype(BF16)
        sent_ref[...] = far_sum
        s_buf[:part, :] = near_sum.astype(BF16)
        s_buf[part:, :] = far_sum
        for m in range(2):
            hit = chosen(base + (zl ^ (2 * m)) * part, part, row)
            rows = slice(m * part, (m + 1) * part)
            m_buf[rows, :] = m_ref[rows, :] * hit.astype(BF16)
        g = lax.dot_general(m_buf[...], s_buf[...], (((0,), (0,)), ((), ())), preferred_element_type=F32)
        g = g.astype(BF16)
        groups, both = g_ref.shape[0], g_ref.shape[1] // 2
        for i in range(groups):
            for h in range(2):
                start = h * (wide // 2) + i * both
                g_ref[i, h * both : (h + 1) * both, :] = g[start : start + both, :]

    return pl.pallas_call(
        kernel,
        in_specs=[scalars()] + [whole()] * 5,
        out_specs=[whole()] * 3,
        out_shape=[
            jax.ShapeDtypeStruct((part, wide), F32),
            jax.ShapeDtypeStruct((part, wide), BF16),
            jax.ShapeDtypeStruct((16, wide // 16, wide), BF16),
        ],
        scratch_shapes=[pltpu.VMEM((2 * part, wide), BF16), pltpu.VMEM((2 * part, wide), BF16)],
        compiler_params=params(),
        name="contract",
    )(me, pattern, mine, near, far, arrived)


def negate(me, height, pattern, half, arrived):
    part, wide = half.shape
    each = part // 2

    def kernel(me_ref, p_ref, half_ref, in_ref, own_ref, send_ref, off):
        zh, x, y, zl, core = place_of(me_ref[0])
        hit = chosen(((zh * 4 + x) * 4 + y) * height + zl * part, part, p_ref[pl.ds(core, 1), :])
        off[...] = -((half_ref[...] + in_ref[...].astype(F32)) * hit)
        own_ref[...] = off[pl.ds(pl.multiple_of(core * each, 16), each), :].astype(BF16)
        send_ref[...] = off[pl.ds(pl.multiple_of((1 - core) * each, 16), each), :].astype(BF16)

    piece = jax.ShapeDtypeStruct((each, wide), BF16)
    return pl.pallas_call(
        kernel,
        in_specs=[scalars()] + [whole()] * 3,
        out_specs=[whole()] * 2,
        out_shape=[piece, piece],
        scratch_shapes=[pltpu.VMEM((part, wide), F32)],
        compiler_params=params(),
        name="negate",
    )(me, pattern, half, arrived)


def gather(pieces):
    count, tall, wide = pieces.shape

    def kernel(in_ref, o_ref):
        total = in_ref[0].astype(F32)
        for i in range(1, count):
            total = total + in_ref[i].astype(F32)
        for j in range(tall // 2):
            o_ref[j] = total[2 * j : 2 * j + 2, :].astype(o_ref.dtype)

    return pl.pallas_call(
        kernel,
        in_specs=[whole()],
        out_specs=whole(),
        out_shape=jax.ShapeDtypeStruct((tall // 2, 2, wide), F32),
        compiler_params=params(),
        name="gather",
    )(pieces)


def finish(pieces, diag):
    def kernel(in_ref, d_ref, o_ref):
        for s in range(2):
            total = in_ref[s]
            for i in range(s + 2, in_ref.shape[0], 2):
                total = total + in_ref[i]
            o_ref[s] = d_ref[s] + total

    return pl.pallas_call(
        kernel,
        in_specs=[whole(), whole()],
        out_specs=whole(),
        out_shape=jax.ShapeDtypeStruct(diag.shape, F32),
        compiler_params=params(),
        name="finish",
    )(pieces, diag)


def solution(mesh):
    cut = Mesh(mesh.devices.reshape(2, 4, 4, 4, 2), ("zh", "x", "y", "zl", "c"))
    every = ("zh", "x", "y", "zl", "c")
    xor4 = {m: [(i, i ^ m) for i in range(4)] for m in (1, 2)}
    swap = [(0, 1), (1, 0)]
    fetch = []
    for source in range(256):
        zh, x, y, p = source >> 7, (source >> 5) & 3, (source >> 3) & 3, source & 7
        fetch.append((source, (p * 4 + y) * 8 + ROUTES[p][zh * 4 + x]))

    def local(ancestor, panel, pattern, diag):
        me = jnp.reshape(lax.axis_index(every), (1,))
        core = lax.axis_index("c")
        height = ancestor.shape[0]
        mine = lax.ppermute(pick(me, height, panel), every, fetch)
        other, own = products(me, ancestor, panel, pattern)
        swapped = lax.ppermute(other, "c", swap)
        near, far, sent = join(me, own, swapped)
        arrived = lax.ppermute(sent, "zl", xor4[1])
        half, sent, g = contract(me, height, pattern, mine, near, far, arrived)
        arrived = lax.ppermute(sent, "zl", xor4[2])
        pieces = lax.all_to_all(g, ("x", "y"), 0, 0, tiled=True)
        off_own, off_send = negate(me, height, pattern, half, arrived)
        off_other = lax.ppermute(off_send, "c", swap)
        off = jnp.where(core == 0, jnp.stack([off_own, off_other]), jnp.stack([off_other, off_own]))
        pieces = lax.all_to_all(gather(pieces), ("zh", "zl", "c"), 0, 0, tiled=True)
        return off, finish(pieces, diag)

    rows = ("zh", "x", "y")
    cols = ("zl", "c")
    return jax.shard_map(
        local,
        mesh=cut,
        in_specs=(P(rows, cols), P(None, cols, None), P(), P(None, every, None)),
        out_specs=(P(None, every, None), P(None, every, None)),
        check_vma=False,
    )
```

```python
import jax
import jax.numpy as jnp
import numpy as np
from jax import lax
from jax.experimental import pallas as pl
from jax.experimental.pallas import tpu as pltpu
from jax.sharding import Mesh
from jax.sharding import PartitionSpec as P

BLOCK = 128
VMEM = pltpu.VMEM
BF16 = jnp.bfloat16
F32 = jnp.float32


def params(mib=40):
    return pltpu.CompilerParams(vmem_limit_bytes=mib * 1024 * 1024)


def whole():
    return pl.BlockSpec(memory_space=VMEM)


def scalars():
    return pl.BlockSpec(memory_space=pltpu.SMEM)


def place_of(me):
    return me >> 7, (me >> 5) & 3, (me >> 3) & 3, (me >> 1) & 3, me & 1


def masked(rows, hits):
    parts = []
    for b in range(rows.shape[0] // BLOCK):
        parts.append(rows[b * BLOCK : (b + 1) * BLOCK, :] * hits[b : b + 1, :].astype(BF16))
    return jnp.concatenate(parts, axis=0)


def hbm():
    return pl.BlockSpec(memory_space=pltpu.HBM)


STEP = 512
LIMIT = 48
ROUTES = (
    (1, 4, 2, 3, 7, 6, 5, 0),
    (4, 3, 2, 1, 0, 5, 7, 6),
    (3, 5, 4, 2, 7, 0, 6, 1),
    (4, 2, 3, 5, 1, 6, 0, 7),
    (1, 7, 6, 0, 2, 5, 4, 3),
    (7, 1, 0, 6, 4, 2, 3, 5),
    (0, 2, 6, 1, 5, 4, 7, 3),
    (1, 7, 0, 2, 6, 3, 5, 4),
)


def cost(height, breadth, wide):
    return pl.CostEstimate(
        flops=2 * height * breadth * wide,
        bytes_accessed=2 * (height * breadth + breadth * wide + height * wide),
        transcendentals=0,
    )


def hits_of(pattern_row, first, blocks):
    ids = first + lax.broadcasted_iota(jnp.int32, (blocks, 1), 0)
    return jnp.max(jnp.where(ids == pattern_row, 1.0, 0.0).astype(F32), axis=1, keepdims=True)


def product_sent(me, ancestor, panel, pattern):
    height, breadth = ancestor.shape
    wide = panel.shape[2]
    steps = breadth // STEP
    part = height // 4
    each = STEP // BLOCK

    def kernel(me_ref, a_hbm, l_hbm, p_hbm, o_ref, a_ref, f_ref, p_ref, l_buf, acc, a_sem, l_sem, f_sem, p_sem):
        zh, x, y, zl, c = place_of(me_ref[0])
        s = 1 - c
        listed = pltpu.make_async_copy(p_hbm, p_ref, p_sem)
        listed.start()
        copies = []
        for k in range(steps):
            cols = pl.ds(k * STEP, STEP)
            copies.append(
                (
                    pltpu.make_async_copy(a_hbm.at[:, cols], a_ref.at[:, cols], a_sem.at[k]),
                    pltpu.make_async_copy(l_hbm.at[s, cols, :], l_buf.at[k], l_sem.at[k]),
                )
            )
            for copy in copies[k]:
                copy.start()
        code = jnp.int32(0)
        for p, row in enumerate(ROUTES):
            code = jnp.where(zl * 2 + c == p, sum(v << (3 * q) for q, v in enumerate(row)), code)
        to = (code >> (3 * (zh * 4 + x))) & 7
        fetches = []
        for m in range(2):
            start = pl.multiple_of(y * height + ((to >> 1) ^ (2 * m)) * part, 16)
            fetches.append(
                pltpu.make_async_copy(
                    l_hbm.at[to & 1, pl.ds(start, part), :], f_ref.at[pl.ds(m * part, part), :], f_sem.at[m]
                )
            )
            fetches[m].start()
        listed.wait()
        hits = hits_of(p_ref[pl.ds(s, 1), :], (zl * 2 + c) * (breadth // BLOCK), breadth // BLOCK)
        for k in range(steps):
            for copy in copies[k]:
                copy.wait()
            rows = masked(l_buf[k], hits[k * each : (k + 1) * each, :])
            term = jnp.dot(a_ref[:, k * STEP : (k + 1) * STEP], rows, preferred_element_type=F32)
            if k == 0:
                acc[...] = term
            elif k < steps - 1:
                acc[...] += term
            else:
                o_ref[...] = (acc[...] + term).astype(BF16)
        for copy in fetches:
            copy.wait()

    return pl.pallas_call(
        kernel,
        in_specs=[scalars(), hbm(), hbm(), hbm()],
        out_specs=[whole(), whole(), whole()],
        out_shape=[
            jax.ShapeDtypeStruct((height, wide), BF16),
            jax.ShapeDtypeStruct((height, breadth), BF16),
            jax.ShapeDtypeStruct((2 * part, wide), BF16),
        ],
        scratch_shapes=[
            pltpu.VMEM(pattern.shape, pattern.dtype),
            pltpu.VMEM((steps, STEP, wide), BF16),
            pltpu.VMEM((height, wide), F32),
            pltpu.SemaphoreType.DMA((steps,)),
            pltpu.SemaphoreType.DMA((steps,)),
            pltpu.SemaphoreType.DMA((2,)),
            pltpu.SemaphoreType.DMA,
        ],
        compiler_params=params(LIMIT),
        cost_estimate=cost(height, breadth, wide),
        name="product_sent",
    )(me, ancestor, panel, pattern)


def product_kept(me, ancestor, panel, pattern):
    height, breadth = ancestor.shape
    wide = panel.shape[2]
    steps = breadth // STEP
    each = STEP // BLOCK

    def kernel(me_ref, a_ref, l_hbm, p_ref, o_ref, l_buf, l_sem):
        zh, x, y, zl, s = place_of(me_ref[0])
        copies = []
        for k in range(steps):
            rows = pl.ds(k * STEP, STEP)
            copies.append(pltpu.make_async_copy(l_hbm.at[s, rows, :], l_buf.at[k], l_sem.at[k]))
            copies[k].start()
        hits = hits_of(p_ref[pl.ds(s, 1), :], (zl * 2 + s) * (breadth // BLOCK), breadth // BLOCK)
        for k in range(steps):
            copies[k].wait()
            rows = masked(l_buf[k], hits[k * each : (k + 1) * each, :])
            term = jnp.dot(a_ref[:, k * STEP : (k + 1) * STEP], rows, preferred_element_type=F32)
            if k == 0:
                o_ref[...] = term
            else:
                o_ref[...] += term

    return pl.pallas_call(
        kernel,
        in_specs=[scalars(), whole(), hbm(), whole()],
        out_specs=whole(),
        out_shape=jax.ShapeDtypeStruct((height, wide), F32),
        scratch_shapes=[pltpu.VMEM((steps, STEP, wide), BF16), pltpu.SemaphoreType.DMA((steps,))],
        compiler_params=params(LIMIT),
        cost_estimate=cost(height, breadth, wide),
        name="product_kept",
    )(me, ancestor, panel, pattern)


def join(me, own, arrived):
    height, wide = own.shape
    part = height // 4

    def kernel(me_ref, own_ref, in_ref, near_ref, far_ref, sent_ref):
        here = place_of(me_ref[0])[3]
        for m in range(4):
            rows = pl.ds(pl.multiple_of((here ^ m) * part, 16), part)
            total = own_ref[rows, :] + in_ref[rows, :].astype(F32)
            if m == 0:
                near_ref[...] = total
            elif m == 2:
                far_ref[...] = total
            else:
                sent_ref[(m // 2) * part : (m // 2 + 1) * part, :] = total.astype(BF16)

    piece = jax.ShapeDtypeStruct((part, wide), F32)
    return pl.pallas_call(
        kernel,
        in_specs=[scalars(), whole(), whole()],
        out_specs=[whole()] * 3,
        out_shape=[piece, piece, jax.ShapeDtypeStruct((2 * part, wide), BF16)],
        compiler_params=params(),
        name="join",
    )(me, own, arrived)


def chosen(first, count, pattern_row):
    ids = (first + lax.broadcasted_iota(jnp.int32, (count, 1), 0)) >> 7
    return jnp.max(jnp.where(ids == pattern_row, 1.0, 0.0).astype(F32), axis=1, keepdims=True)


def contract(me, height, pattern, mine, near, far, arrived):
    part, wide = near.shape

    def kernel(me_ref, p_ref, m_ref, near_ref, far_ref, in_ref, half_ref, sent_ref, g_ref, m_buf, s_buf):
        zh, x, y, zl, core = place_of(me_ref[0])
        row = p_ref[pl.ds(core, 1), :]
        base = ((zh * 4 + x) * 4 + y) * height
        near_sum = near_ref[...] + in_ref[:part, :].astype(F32)
        half_ref[...] = near_sum
        far_sum = (far_ref[...] + in_ref[part:, :].astype(F32)).astype(BF16)
        sent_ref[...] = far_sum
        s_buf[:part, :] = near_sum.astype(BF16)
        s_buf[part:, :] = far_sum
        for m in range(2):
            hit = chosen(base + (zl ^ (2 * m)) * part, part, row)
            rows = slice(m * part, (m + 1) * part)
            m_buf[rows, :] = m_ref[rows, :] * hit.astype(BF16)
        g = lax.dot_general(m_buf[...], s_buf[...], (((0,), (0,)), ((), ())), preferred_element_type=F32)
        g = g.astype(BF16)
        groups, both = g_ref.shape[0], g_ref.shape[1] // 2
        for i in range(groups):
            for h in range(2):
                start = h * (wide // 2) + i * both
                g_ref[i, h * both : (h + 1) * both, :] = g[start : start + both, :]

    return pl.pallas_call(
        kernel,
        in_specs=[scalars()] + [whole()] * 5,
        out_specs=[whole()] * 3,
        out_shape=[
            jax.ShapeDtypeStruct((part, wide), F32),
            jax.ShapeDtypeStruct((part, wide), BF16),
            jax.ShapeDtypeStruct((16, wide // 16, wide), BF16),
        ],
        scratch_shapes=[pltpu.VMEM((2 * part, wide), BF16), pltpu.VMEM((2 * part, wide), BF16)],
        compiler_params=params(),
        name="contract",
    )(me, pattern, mine, near, far, arrived)


def negate(me, height, pattern, half, arrived, after):
    part, wide = half.shape
    each = part // 2

    def kernel(me_ref, p_ref, half_ref, in_ref, after_ref, own_ref, send_ref, off):
        zh, x, y, zl, core = place_of(me_ref[0])
        hit = chosen(((zh * 4 + x) * 4 + y) * height + zl * part, part, p_ref[pl.ds(core, 1), :])
        off[...] = -((half_ref[...] + in_ref[...].astype(F32)) * hit)
        own_ref[...] = off[pl.ds(pl.multiple_of(core * each, 16), each), :].astype(BF16)
        send_ref[...] = off[pl.ds(pl.multiple_of((1 - core) * each, 16), each), :].astype(BF16)

    piece = jax.ShapeDtypeStruct((each, wide), BF16)
    return pl.pallas_call(
        kernel,
        in_specs=[scalars()] + [whole()] * 3 + [pl.BlockSpec(memory_space=pl.ANY)],
        out_specs=[whole()] * 2,
        out_shape=[piece, piece],
        scratch_shapes=[pltpu.VMEM((part, wide), F32)],
        compiler_params=params(),
        name="negate",
    )(me, pattern, half, arrived, after)


def gather(pieces):
    count, tall, wide = pieces.shape

    def kernel(in_ref, o_ref):
        total = in_ref[0].astype(F32)
        for i in range(1, count):
            total = total + in_ref[i].astype(F32)
        for j in range(tall // 2):
            o_ref[j] = total[2 * j : 2 * j + 2, :].astype(o_ref.dtype)

    return pl.pallas_call(
        kernel,
        in_specs=[whole()],
        out_specs=whole(),
        out_shape=jax.ShapeDtypeStruct((tall // 2, 2, wide), F32),
        compiler_params=params(),
        name="gather",
    )(pieces)


def finish(pieces, diag):
    def kernel(in_ref, d_ref, o_ref):
        for s in range(2):
            total = in_ref[s]
            for i in range(s + 2, in_ref.shape[0], 2):
                total = total + in_ref[i]
            o_ref[s] = d_ref[s] + total

    return pl.pallas_call(
        kernel,
        in_specs=[whole(), whole()],
        out_specs=whole(),
        out_shape=jax.ShapeDtypeStruct(diag.shape, F32),
        compiler_params=params(),
        name="finish",
    )(pieces, diag)


def solution(mesh):
    cut = Mesh(mesh.devices.reshape(2, 4, 4, 4, 2), ("zh", "x", "y", "zl", "c"))
    every = ("zh", "x", "y", "zl", "c")
    xor4 = {m: [(i, i ^ m) for i in range(4)] for m in (1, 2)}
    swap = [(0, 1), (1, 0)]
    fetch = []
    for source in range(256):
        zh, x, y, p = source >> 7, (source >> 5) & 3, (source >> 3) & 3, source & 7
        fetch.append((source, (p * 4 + y) * 8 + ROUTES[p][zh * 4 + x]))

    def local(ancestor, panel, pattern, diag):
        me = jnp.reshape(lax.axis_index(every), (1,))
        core = lax.axis_index("c")
        height = ancestor.shape[0]
        other, held, picked = product_sent(me, ancestor, panel, pattern)
        swapped = lax.ppermute(other, "c", swap)
        mine = lax.ppermute(picked, every, fetch)
        own = product_kept(me, held, panel, pattern)
        near, far, sent = join(me, own, swapped)
        arrived = lax.ppermute(sent, "zl", xor4[1])
        half, sent, g = contract(me, height, pattern, mine, near, far, arrived)
        arrived = lax.ppermute(sent, "zl", xor4[2])
        pieces = lax.all_to_all(g, ("x", "y"), 0, 0, tiled=True)
        gathered = gather(pieces)
        off_own, off_send = negate(me, height, pattern, half, arrived, gathered)
        off_other = lax.ppermute(off_send, "c", swap)
        off = jnp.where(core == 0, jnp.stack([off_own, off_other]), jnp.stack([off_other, off_own]))
        pieces = lax.all_to_all(gathered, ("zh", "zl", "c"), 0, 0, tiled=True)
        return off, finish(pieces, diag)

    rows = ("zh", "x", "y")
    cols = ("zl", "c")
    return jax.shard_map(
        local,
        mesh=cut,
        in_specs=(P(rows, cols), P(None, cols, None), P(), P(None, every, None)),
        out_specs=(P(None, every, None), P(None, every, None)),
        check_vma=False,
    )
```

```python
import jax
import jax.numpy as jnp
import numpy as np
from jax import lax
from jax.experimental import pallas as pl
from jax.experimental.pallas import tpu as pltpu
from jax.sharding import Mesh
from jax.sharding import PartitionSpec as P

BLOCK = 128
VMEM = pltpu.VMEM
BF16 = jnp.bfloat16
F32 = jnp.float32


def params(mib=40):
    return pltpu.CompilerParams(vmem_limit_bytes=mib * 1024 * 1024)


def whole():
    return pl.BlockSpec(memory_space=VMEM)


def scalars():
    return pl.BlockSpec(memory_space=pltpu.SMEM)


def place_of(me):
    return me >> 7, (me >> 5) & 3, (me >> 3) & 3, (me >> 1) & 3, me & 1


def masked(rows, hits):
    parts = []
    for b in range(rows.shape[0] // BLOCK):
        parts.append(rows[b * BLOCK : (b + 1) * BLOCK, :] * hits[b : b + 1, :].astype(BF16))
    return jnp.concatenate(parts, axis=0)


def hbm():
    return pl.BlockSpec(memory_space=pltpu.HBM)


STEP = 512
LIMIT = 48
ROUTES = (
    (1, 4, 2, 3, 7, 6, 5, 0),
    (4, 3, 2, 1, 0, 5, 7, 6),
    (3, 5, 4, 2, 7, 0, 6, 1),
    (4, 2, 3, 5, 1, 6, 0, 7),
    (1, 7, 6, 0, 2, 5, 4, 3),
    (7, 1, 0, 6, 4, 2, 3, 5),
    (0, 2, 6, 1, 5, 4, 7, 3),
    (1, 7, 0, 2, 6, 3, 5, 4),
)


def cost(height, breadth, wide):
    return pl.CostEstimate(
        flops=2 * height * breadth * wide,
        bytes_accessed=2 * (height * breadth + breadth * wide + height * wide),
        transcendentals=0,
    )


def hits_of(pattern_row, first, blocks):
    ids = first + lax.broadcasted_iota(jnp.int32, (blocks, 1), 0)
    return jnp.max(jnp.where(ids == pattern_row, 1.0, 0.0).astype(F32), axis=1, keepdims=True)


def product_sent(me, ancestor, panel, pattern):
    height, breadth = ancestor.shape
    wide = panel.shape[2]
    steps = breadth // STEP
    part = height // 4
    each = STEP // BLOCK

    def kernel(me_ref, a_hbm, l_hbm, p_hbm, o_ref, a_ref, f_ref, p_ref, l_buf, acc, a_sem, l_sem, f_sem, p_sem):
        zh, x, y, zl, c = place_of(me_ref[0])
        s = 1 - c
        listed = pltpu.make_async_copy(p_hbm, p_ref, p_sem)
        listed.start()
        copies = []
        for k in range(steps):
            cols = pl.ds(k * STEP, STEP)
            copies.append(
                (
                    pltpu.make_async_copy(a_hbm.at[:, cols], a_ref.at[:, cols], a_sem.at[k]),
                    pltpu.make_async_copy(l_hbm.at[s, cols, :], l_buf.at[k], l_sem.at[k]),
                )
            )
            for copy in copies[k]:
                copy.start()
        code = jnp.int32(0)
        for p, row in enumerate(ROUTES):
            code = jnp.where(zl * 2 + c == p, sum(v << (3 * q) for q, v in enumerate(row)), code)
        to = (code >> (3 * (zh * 4 + x))) & 7
        fetches = []
        for m in range(2):
            start = pl.multiple_of(y * height + ((to >> 1) ^ (2 * m)) * part, 16)
            fetches.append(
                pltpu.make_async_copy(
                    l_hbm.at[to & 1, pl.ds(start, part), :], f_ref.at[pl.ds(m * part, part), :], f_sem.at[m]
                )
            )
            fetches[m].start()
        listed.wait()
        hits = hits_of(p_ref[pl.ds(s, 1), :], (zl * 2 + c) * (breadth // BLOCK), breadth // BLOCK)
        for k in range(steps):
            for copy in copies[k]:
                copy.wait()
            rows = masked(l_buf[k], hits[k * each : (k + 1) * each, :])
            term = jnp.dot(a_ref[:, k * STEP : (k + 1) * STEP], rows, preferred_element_type=F32)
            if k == 0:
                acc[...] = term
            elif k < steps - 1:
                acc[...] += term
            else:
                o_ref[...] = (acc[...] + term).astype(BF16)
        for copy in fetches:
            copy.wait()

    return pl.pallas_call(
        kernel,
        in_specs=[scalars(), hbm(), hbm(), hbm()],
        out_specs=[whole(), whole(), whole()],
        out_shape=[
            jax.ShapeDtypeStruct((height, wide), BF16),
            jax.ShapeDtypeStruct((height, breadth), BF16),
            jax.ShapeDtypeStruct((2 * part, wide), BF16),
        ],
        scratch_shapes=[
            pltpu.VMEM(pattern.shape, pattern.dtype),
            pltpu.VMEM((steps, STEP, wide), BF16),
            pltpu.VMEM((height, wide), F32),
            pltpu.SemaphoreType.DMA((steps,)),
            pltpu.SemaphoreType.DMA((steps,)),
            pltpu.SemaphoreType.DMA((2,)),
            pltpu.SemaphoreType.DMA,
        ],
        compiler_params=params(LIMIT),
        cost_estimate=cost(height, breadth, wide),
        name="product_sent",
    )(me, ancestor, panel, pattern)


def product_rows(me, ancestor, panel, pattern, arrived, quarters):
    height, breadth = ancestor.shape
    wide = panel.shape[2]
    steps = breadth // STEP
    each = STEP // BLOCK
    part = height // 4
    sent = 0 not in quarters

    def kernel(me_ref, a_ref, l_hbm, p_ref, in_ref, *rest):
        outs, (l_buf, acc, l_sem) = rest[:-3], rest[-3:]
        zh, x, y, zl, s = place_of(me_ref[0])
        copies = []
        for k in range(steps):
            rows = pl.ds(k * STEP, STEP)
            copies.append(pltpu.make_async_copy(l_hbm.at[s, rows, :], l_buf.at[k], l_sem.at[k]))
            copies[k].start()
        hits = hits_of(p_ref[pl.ds(s, 1), :], (zl * 2 + s) * (breadth // BLOCK), breadth // BLOCK)
        places = [pl.ds(pl.multiple_of((zl ^ m) * part, 16), part) for m in quarters]
        for i, at in enumerate(places):
            acc[i * part : (i + 1) * part, :] = in_ref[at, :].astype(F32)
        for k in range(steps):
            copies[k].wait()
            right = masked(l_buf[k], hits[k * each : (k + 1) * each, :])
            left = jnp.concatenate([a_ref[at, k * STEP : (k + 1) * STEP] for at in places], axis=0)
            acc[...] += jnp.dot(left, right, preferred_element_type=F32)
        if sent:
            outs[0][...] = acc[...].astype(BF16)
        else:
            for i, out in enumerate(outs):
                out[...] = acc[i * part : (i + 1) * part, :]

    piece = jax.ShapeDtypeStruct((part, wide), F32)
    shapes = [jax.ShapeDtypeStruct((2 * part, wide), BF16)] if sent else [piece, piece]
    return pl.pallas_call(
        kernel,
        in_specs=[scalars(), whole(), hbm(), whole(), whole()],
        out_specs=[whole()] * len(shapes),
        out_shape=shapes,
        scratch_shapes=[
            pltpu.VMEM((steps, STEP, wide), BF16),
            pltpu.VMEM((2 * part, wide), F32),
            pltpu.SemaphoreType.DMA((steps,)),
        ],
        compiler_params=params(LIMIT),
        cost_estimate=cost(height // 2, breadth, wide),
        name="product_rows",
    )(me, ancestor, panel, pattern, arrived)


def chosen(first, count, pattern_row):
    ids = (first + lax.broadcasted_iota(jnp.int32, (count, 1), 0)) >> 7
    return jnp.max(jnp.where(ids == pattern_row, 1.0, 0.0).astype(F32), axis=1, keepdims=True)


def contract(me, height, pattern, mine, near, far, arrived):
    part, wide = near.shape

    def kernel(me_ref, p_ref, m_ref, near_ref, far_ref, in_ref, half_ref, sent_ref, g_ref, m_buf, s_buf):
        zh, x, y, zl, core = place_of(me_ref[0])
        row = p_ref[pl.ds(core, 1), :]
        base = ((zh * 4 + x) * 4 + y) * height
        near_sum = near_ref[...] + in_ref[:part, :].astype(F32)
        half_ref[...] = near_sum
        far_sum = (far_ref[...] + in_ref[part:, :].astype(F32)).astype(BF16)
        sent_ref[...] = far_sum
        s_buf[:part, :] = near_sum.astype(BF16)
        s_buf[part:, :] = far_sum
        for m in range(2):
            hit = chosen(base + (zl ^ (2 * m)) * part, part, row)
            rows = slice(m * part, (m + 1) * part)
            m_buf[rows, :] = m_ref[rows, :] * hit.astype(BF16)
        g = lax.dot_general(m_buf[...], s_buf[...], (((0,), (0,)), ((), ())), preferred_element_type=F32)
        g = g.astype(BF16)
        groups, both = g_ref.shape[0], g_ref.shape[1] // 2
        for i in range(groups):
            for h in range(2):
                start = h * (wide // 2) + i * both
                g_ref[i, h * both : (h + 1) * both, :] = g[start : start + both, :]

    return pl.pallas_call(
        kernel,
        in_specs=[scalars()] + [whole()] * 5,
        out_specs=[whole()] * 3,
        out_shape=[
            jax.ShapeDtypeStruct((part, wide), F32),
            jax.ShapeDtypeStruct((part, wide), BF16),
            jax.ShapeDtypeStruct((16, wide // 16, wide), BF16),
        ],
        scratch_shapes=[pltpu.VMEM((2 * part, wide), BF16), pltpu.VMEM((2 * part, wide), BF16)],
        compiler_params=params(),
        name="contract",
    )(me, pattern, mine, near, far, arrived)


def negate(me, height, pattern, half, arrived, after):
    part, wide = half.shape
    each = part // 2

    def kernel(me_ref, p_ref, half_ref, in_ref, after_ref, own_ref, send_ref, off):
        zh, x, y, zl, core = place_of(me_ref[0])
        hit = chosen(((zh * 4 + x) * 4 + y) * height + zl * part, part, p_ref[pl.ds(core, 1), :])
        off[...] = -((half_ref[...] + in_ref[...].astype(F32)) * hit)
        own_ref[...] = off[pl.ds(pl.multiple_of(core * each, 16), each), :].astype(BF16)
        send_ref[...] = off[pl.ds(pl.multiple_of((1 - core) * each, 16), each), :].astype(BF16)

    piece = jax.ShapeDtypeStruct((each, wide), BF16)
    return pl.pallas_call(
        kernel,
        in_specs=[scalars()] + [whole()] * 3 + [pl.BlockSpec(memory_space=pl.ANY)],
        out_specs=[whole()] * 2,
        out_shape=[piece, piece],
        scratch_shapes=[pltpu.VMEM((part, wide), F32)],
        compiler_params=params(),
        name="negate",
    )(me, pattern, half, arrived, after)


def gather(pieces):
    count, tall, wide = pieces.shape

    def kernel(in_ref, o_ref):
        total = in_ref[0].astype(F32)
        for i in range(1, count):
            total = total + in_ref[i].astype(F32)
        for j in range(tall // 2):
            o_ref[j] = total[2 * j : 2 * j + 2, :].astype(o_ref.dtype)

    return pl.pallas_call(
        kernel,
        in_specs=[whole()],
        out_specs=whole(),
        out_shape=jax.ShapeDtypeStruct((tall // 2, 2, wide), F32),
        compiler_params=params(),
        name="gather",
    )(pieces)


def finish(pieces, diag):
    def kernel(in_ref, d_ref, o_ref):
        for s in range(2):
            total = in_ref[s]
            for i in range(s + 2, in_ref.shape[0], 2):
                total = total + in_ref[i]
            o_ref[s] = d_ref[s] + total

    return pl.pallas_call(
        kernel,
        in_specs=[whole(), whole()],
        out_specs=whole(),
        out_shape=jax.ShapeDtypeStruct(diag.shape, F32),
        compiler_params=params(),
        name="finish",
    )(pieces, diag)


def solution(mesh):
    cut = Mesh(mesh.devices.reshape(2, 4, 4, 4, 2), ("zh", "x", "y", "zl", "c"))
    every = ("zh", "x", "y", "zl", "c")
    xor4 = {m: [(i, i ^ m) for i in range(4)] for m in (1, 2)}
    swap = [(0, 1), (1, 0)]
    fetch = []
    for source in range(256):
        zh, x, y, p = source >> 7, (source >> 5) & 3, (source >> 3) & 3, source & 7
        fetch.append((source, (p * 4 + y) * 8 + ROUTES[p][zh * 4 + x]))

    def local(ancestor, panel, pattern, diag):
        me = jnp.reshape(lax.axis_index(every), (1,))
        core = lax.axis_index("c")
        height = ancestor.shape[0]
        other, held, picked = product_sent(me, ancestor, panel, pattern)
        swapped = lax.ppermute(other, "c", swap)
        mine = lax.ppermute(picked, every, fetch)
        (sent,) = product_rows(me, held, panel, pattern, swapped, (1, 3))
        arrived = lax.ppermute(sent, "zl", xor4[1])
        near, far = product_rows(me, held, panel, pattern, swapped, (0, 2))
        half, sent, g = contract(me, height, pattern, mine, near, far, arrived)
        arrived = lax.ppermute(sent, "zl", xor4[2])
        pieces = lax.all_to_all(g, ("x", "y"), 0, 0, tiled=True)
        gathered = gather(pieces)
        off_own, off_send = negate(me, height, pattern, half, arrived, gathered)
        off_other = lax.ppermute(off_send, "c", swap)
        off = jnp.where(core == 0, jnp.stack([off_own, off_other]), jnp.stack([off_other, off_own]))
        pieces = lax.all_to_all(gathered, ("zh", "zl", "c"), 0, 0, tiled=True)
        return off, finish(pieces, diag)

    rows = ("zh", "x", "y")
    cols = ("zl", "c")
    return jax.shard_map(
        local,
        mesh=cut,
        in_specs=(P(rows, cols), P(None, cols, None), P(), P(None, every, None)),
        out_specs=(P(None, every, None), P(None, every, None)),
        check_vma=False,
    )
```

```python
import jax
import jax.numpy as jnp
import numpy as np
from jax import lax
from jax.experimental import pallas as pl
from jax.experimental.pallas import tpu as pltpu
from jax.sharding import Mesh
from jax.sharding import PartitionSpec as P

BLOCK = 128
VMEM = pltpu.VMEM
BF16 = jnp.bfloat16
F32 = jnp.float32


def params(mib=40):
    return pltpu.CompilerParams(vmem_limit_bytes=mib * 1024 * 1024)


def whole():
    return pl.BlockSpec(memory_space=VMEM)


def scalars():
    return pl.BlockSpec(memory_space=pltpu.SMEM)


def place_of(me):
    return me >> 7, (me >> 5) & 3, (me >> 3) & 3, (me >> 1) & 3, me & 1


def masked(rows, hits):
    parts = []
    for b in range(rows.shape[0] // BLOCK):
        parts.append(rows[b * BLOCK : (b + 1) * BLOCK, :] * hits[b : b + 1, :].astype(BF16))
    return jnp.concatenate(parts, axis=0)


def hbm():
    return pl.BlockSpec(memory_space=pltpu.HBM)


STEP = 512
LIMIT = 48
ROUTES = (
    (1, 4, 2, 3, 7, 6, 5, 0),
    (4, 3, 2, 1, 0, 5, 7, 6),
    (3, 5, 4, 2, 7, 0, 6, 1),
    (4, 2, 3, 5, 1, 6, 0, 7),
    (1, 7, 6, 0, 2, 5, 4, 3),
    (7, 1, 0, 6, 4, 2, 3, 5),
    (0, 2, 6, 1, 5, 4, 7, 3),
    (1, 7, 0, 2, 6, 3, 5, 4),
)


def cost(height, breadth, wide):
    return pl.CostEstimate(
        flops=2 * height * breadth * wide,
        bytes_accessed=2 * (height * breadth + breadth * wide + height * wide),
        transcendentals=0,
    )


def hits_of(pattern_row, first, blocks):
    ids = first + lax.broadcasted_iota(jnp.int32, (blocks, 1), 0)
    return jnp.max(jnp.where(ids == pattern_row, 1.0, 0.0).astype(F32), axis=1, keepdims=True)


def product_sent(me, ancestor, panel, pattern):
    height, breadth = ancestor.shape
    wide = panel.shape[2]
    steps = breadth // STEP
    part = height // 4
    each = STEP // BLOCK

    def kernel(me_ref, a_hbm, l_hbm, p_hbm, o_ref, a_ref, f_ref, p_ref, l_buf, acc, a_sem, l_sem, f_sem, p_sem):
        zh, x, y, zl, c = place_of(me_ref[0])
        s = 1 - c
        listed = pltpu.make_async_copy(p_hbm, p_ref, p_sem)
        listed.start()
        copies = []
        for k in range(steps):
            cols = pl.ds(k * STEP, STEP)
            copies.append(
                (
                    pltpu.make_async_copy(a_hbm.at[:, cols], a_ref.at[:, cols], a_sem.at[k]),
                    pltpu.make_async_copy(l_hbm.at[s, cols, :], l_buf.at[k], l_sem.at[k]),
                )
            )
            for copy in copies[k]:
                copy.start()
        code = jnp.int32(0)
        for p, row in enumerate(ROUTES):
            code = jnp.where(zl * 2 + c == p, sum(v << (3 * q) for q, v in enumerate(row)), code)
        to = (code >> (3 * (zh * 4 + x))) & 7
        fetches = []
        for m in range(2):
            start = pl.multiple_of(y * height + ((to >> 1) ^ (2 * m)) * part, 16)
            fetches.append(
                pltpu.make_async_copy(
                    l_hbm.at[to & 1, pl.ds(start, part), :], f_ref.at[pl.ds(m * part, part), :], f_sem.at[m]
                )
            )
            fetches[m].start()
        listed.wait()
        hits = hits_of(p_ref[pl.ds(s, 1), :], (zl * 2 + c) * (breadth // BLOCK), breadth // BLOCK)
        for k in range(steps):
            for copy in copies[k]:
                copy.wait()
            rows = masked(l_buf[k], hits[k * each : (k + 1) * each, :])
            term = jnp.dot(a_ref[:, k * STEP : (k + 1) * STEP], rows, preferred_element_type=F32)
            if k == 0:
                acc[...] = term
            elif k < steps - 1:
                acc[...] += term
            else:
                o_ref[...] = (acc[...] + term).astype(BF16)
        for copy in fetches:
            copy.wait()

    return pl.pallas_call(
        kernel,
        in_specs=[scalars(), hbm(), hbm(), hbm()],
        out_specs=[whole(), whole(), whole()],
        out_shape=[
            jax.ShapeDtypeStruct((height, wide), BF16),
            jax.ShapeDtypeStruct((height, breadth), BF16),
            jax.ShapeDtypeStruct((2 * part, wide), BF16),
        ],
        scratch_shapes=[
            pltpu.VMEM(pattern.shape, pattern.dtype),
            pltpu.VMEM((steps, STEP, wide), BF16),
            pltpu.VMEM((height, wide), F32),
            pltpu.SemaphoreType.DMA((steps,)),
            pltpu.SemaphoreType.DMA((steps,)),
            pltpu.SemaphoreType.DMA((2,)),
            pltpu.SemaphoreType.DMA,
        ],
        compiler_params=params(LIMIT),
        cost_estimate=cost(height, breadth, wide),
        name="product_sent",
    )(me, ancestor, panel, pattern)


def product_rows(me, ancestor, panel, pattern, arrived, quarters):
    height, breadth = ancestor.shape
    wide = panel.shape[2]
    steps = breadth // STEP
    each = STEP // BLOCK
    part = height // 4
    sent = 0 not in quarters

    def kernel(me_ref, a_ref, l_hbm, p_ref, in_ref, *rest):
        outs, (l_buf, acc, l_sem) = rest[:-3], rest[-3:]
        zh, x, y, zl, s = place_of(me_ref[0])
        copies = []
        for k in range(steps):
            rows = pl.ds(k * STEP, STEP)
            copies.append(pltpu.make_async_copy(l_hbm.at[s, rows, :], l_buf.at[k], l_sem.at[k]))
            copies[k].start()
        hits = hits_of(p_ref[pl.ds(s, 1), :], (zl * 2 + s) * (breadth // BLOCK), breadth // BLOCK)
        places = [pl.ds(pl.multiple_of((zl ^ m) * part, 16), part) for m in quarters]
        for i, at in enumerate(places):
            acc[i * part : (i + 1) * part, :] = in_ref[at, :].astype(F32)
        for k in range(steps):
            copies[k].wait()
            right = masked(l_buf[k], hits[k * each : (k + 1) * each, :])
            left = jnp.concatenate([a_ref[at, k * STEP : (k + 1) * STEP] for at in places], axis=0)
            acc[...] += jnp.dot(left, right, preferred_element_type=F32)
        if sent:
            outs[0][...] = acc[...].astype(BF16)
        else:
            for i, out in enumerate(outs):
                out[...] = acc[i * part : (i + 1) * part, :]

    piece = jax.ShapeDtypeStruct((part, wide), F32)
    shapes = [jax.ShapeDtypeStruct((2 * part, wide), BF16)] if sent else [piece, piece]
    return pl.pallas_call(
        kernel,
        in_specs=[scalars(), whole(), hbm(), whole(), whole()],
        out_specs=[whole()] * len(shapes),
        out_shape=shapes,
        scratch_shapes=[
            pltpu.VMEM((steps, STEP, wide), BF16),
            pltpu.VMEM((2 * part, wide), F32),
            pltpu.SemaphoreType.DMA((steps,)),
        ],
        compiler_params=params(LIMIT),
        cost_estimate=cost(height // 2, breadth, wide),
        name="product_rows",
    )(me, ancestor, panel, pattern, arrived)


def chosen(first, count, pattern_row):
    ids = (first + lax.broadcasted_iota(jnp.int32, (count, 1), 0)) >> 7
    return jnp.max(jnp.where(ids == pattern_row, 1.0, 0.0).astype(F32), axis=1, keepdims=True)


def contract(me, height, pattern, mine, near, far, arrived):
    part, wide = near.shape

    def kernel(me_ref, p_ref, m_ref, near_ref, far_ref, in_ref, half_ref, sent_ref, g_ref, m_buf, s_buf):
        zh, x, y, zl, core = place_of(me_ref[0])
        row = p_ref[pl.ds(core, 1), :]
        base = ((zh * 4 + x) * 4 + y) * height
        near_sum = near_ref[...] + in_ref[:part, :].astype(F32)
        half_ref[...] = near_sum
        far_sum = (far_ref[...] + in_ref[part:, :].astype(F32)).astype(BF16)
        sent_ref[...] = far_sum
        s_buf[:part, :] = near_sum.astype(BF16)
        s_buf[part:, :] = far_sum
        for m in range(2):
            hit = chosen(base + (zl ^ (2 * m)) * part, part, row)
            rows = slice(m * part, (m + 1) * part)
            m_buf[rows, :] = m_ref[rows, :] * hit.astype(BF16)
        g = lax.dot_general(m_buf[...], s_buf[...], (((0,), (0,)), ((), ())), preferred_element_type=F32)
        g = g.astype(BF16)
        groups, both = g_ref.shape[0], g_ref.shape[1] // 2
        for i in range(groups):
            for h in range(2):
                start = h * (wide // 2) + i * both
                g_ref[i, h * both : (h + 1) * both, :] = g[start : start + both, :]

    return pl.pallas_call(
        kernel,
        in_specs=[scalars()] + [whole()] * 5,
        out_specs=[whole()] * 3,
        out_shape=[
            jax.ShapeDtypeStruct((part, wide), F32),
            jax.ShapeDtypeStruct((part, wide), BF16),
            jax.ShapeDtypeStruct((16, wide // 16, wide), BF16),
        ],
        scratch_shapes=[pltpu.VMEM((2 * part, wide), BF16), pltpu.VMEM((2 * part, wide), BF16)],
        compiler_params=params(),
        name="contract",
    )(me, pattern, mine, near, far, arrived)


def negate(me, height, pattern, half, arrived, after):
    part, wide = half.shape
    each = part // 2

    def kernel(me_ref, p_ref, half_ref, in_ref, after_ref, own_ref, send_ref, off):
        zh, x, y, zl, core = place_of(me_ref[0])
        hit = chosen(((zh * 4 + x) * 4 + y) * height + zl * part, part, p_ref[pl.ds(core, 1), :])
        off[...] = -((half_ref[...] + in_ref[...].astype(F32)) * hit)
        own_ref[...] = off[pl.ds(pl.multiple_of(core * each, 16), each), :].astype(BF16)
        send_ref[...] = off[pl.ds(pl.multiple_of((1 - core) * each, 16), each), :].astype(BF16)

    piece = jax.ShapeDtypeStruct((each, wide), BF16)
    return pl.pallas_call(
        kernel,
        in_specs=[scalars()] + [whole()] * 3 + [pl.BlockSpec(memory_space=pl.ANY)],
        out_specs=[whole()] * 2,
        out_shape=[piece, piece],
        scratch_shapes=[pltpu.VMEM((part, wide), F32)],
        compiler_params=params(),
        name="negate",
    )(me, pattern, half, arrived, after)


def assemble(me, own, other):
    def kernel(me_ref, own_ref, other_ref, o_ref):
        core = me_ref[0] & 1
        o_ref[core] = own_ref[...]
        o_ref[1 - core] = other_ref[...]

    return pl.pallas_call(
        kernel,
        in_specs=[scalars(), whole(), whole()],
        out_specs=whole(),
        out_shape=jax.ShapeDtypeStruct((2, *own.shape), own.dtype),
        compiler_params=params(),
        cost_estimate=pl.CostEstimate(flops=1, bytes_accessed=1, transcendentals=0),
        name="assemble",
    )(me, own, other)


def gather(pieces):
    count, tall, wide = pieces.shape

    def kernel(in_ref, o_ref):
        total = in_ref[0].astype(F32)
        for i in range(1, count):
            total = total + in_ref[i].astype(F32)
        for j in range(tall // 2):
            o_ref[j] = total[2 * j : 2 * j + 2, :].astype(o_ref.dtype)

    return pl.pallas_call(
        kernel,
        in_specs=[whole()],
        out_specs=whole(),
        out_shape=jax.ShapeDtypeStruct((tall // 2, 2, wide), F32),
        compiler_params=params(),
        name="gather",
    )(pieces)


def finish(pieces, diag):
    def kernel(in_ref, d_ref, o_ref):
        for s in range(2):
            total = in_ref[s]
            for i in range(s + 2, in_ref.shape[0], 2):
                total = total + in_ref[i]
            o_ref[s] = d_ref[s] + total

    return pl.pallas_call(
        kernel,
        in_specs=[whole(), whole()],
        out_specs=whole(),
        out_shape=jax.ShapeDtypeStruct(diag.shape, F32),
        compiler_params=params(),
        name="finish",
    )(pieces, diag)


def solution(mesh):
    cut = Mesh(mesh.devices.reshape(2, 4, 4, 4, 2), ("zh", "x", "y", "zl", "c"))
    every = ("zh", "x", "y", "zl", "c")
    xor4 = {m: [(i, i ^ m) for i in range(4)] for m in (1, 2)}
    swap = [(0, 1), (1, 0)]
    fetch = []
    for source in range(256):
        zh, x, y, p = source >> 7, (source >> 5) & 3, (source >> 3) & 3, source & 7
        fetch.append((source, (p * 4 + y) * 8 + ROUTES[p][zh * 4 + x]))

    def local(ancestor, panel, pattern, diag):
        me = jnp.reshape(lax.axis_index(every), (1,))
        height = ancestor.shape[0]
        other, held, picked = product_sent(me, ancestor, panel, pattern)
        swapped = lax.ppermute(other, "c", swap)
        mine = lax.ppermute(picked, every, fetch)
        (sent,) = product_rows(me, held, panel, pattern, swapped, (1, 3))
        arrived = lax.ppermute(sent, "zl", xor4[1])
        near, far = product_rows(me, held, panel, pattern, swapped, (0, 2))
        half, sent, g = contract(me, height, pattern, mine, near, far, arrived)
        arrived = lax.ppermute(sent, "zl", xor4[2])
        pieces = lax.all_to_all(g, ("x", "y"), 0, 0, tiled=True)
        gathered = gather(pieces)
        off_own, off_send = negate(me, height, pattern, half, arrived, gathered)
        off_other = lax.ppermute(off_send, "c", swap)
        off = assemble(me, off_own, off_other)
        pieces = lax.all_to_all(gathered, ("zh", "zl", "c"), 0, 0, tiled=True)
        return off, finish(pieces, diag)

    rows = ("zh", "x", "y")
    cols = ("zl", "c")
    return jax.shard_map(
        local,
        mesh=cut,
        in_specs=(P(rows, cols), P(None, cols, None), P(), P(None, every, None)),
        out_specs=(P(None, every, None), P(None, every, None)),
        check_vma=False,
    )
```
